32 devices in a mesh: ctx: 8 (over z, x), head: 4 (over y, core).
Axes of the slice: x: 2, y: 2, z: 4, core: 2. Of those that a mesh axis runs over, the one named last changes fastest.
Arguments:
- query_in: bfloat16 [6144, 20, 128], P(('ctx', 'head')), may hold values from -24 to 24
- key_in: bfloat16 [6144, 20, 128], P(('ctx', 'head')), may hold values from -24 to 24
- value_in: bfloat16 [6144, 20, 128], P(('ctx', 'head')), may hold values from -6 to 6
- grad_out: bfloat16 [6144, 20, 128], P(('ctx', 'head')), may hold values from -6 to 6
- doc_ids: int32 [6144], replicated, may hold values from 0 to 15, never falling along the last dimension, each value on 1 to 768 neighbouring positions
- frame_kind: int32 [96], replicated, may hold values 0 or 1
Outputs:
- attn_output: bfloat16 [6144, 20, 128], P(('ctx', 'head'))
- grad_query: bfloat16 [6144, 20, 128], P(('ctx', 'head'))
- grad_key: bfloat16 [6144, 20, 128], P(('ctx', 'head'))
- grad_value: bfloat16 [6144, 20, 128], P(('ctx', 'head'))
The draws below stay inside these ranges and needn't reach their ends.
Inputs may be any that keep to these rules, and one draw needn't show every extreme that they name: doc_ids never falls along the sequence; every document has 1 to 768 tokens and one has exactly 768.
All inputs are finite; a program needn't handle non-finite values.
Results may differ from the reference program's by a relative error of at most 0.017.
Values may be sent and summed in bfloat16 or wider, within the bound.
No kernel may reach another device: no remote copies, remote signals or barrier semaphores. Data moves between devices by JAX's collectives and lax.ppermute only.
A program may use at most 128 MiB of HBM per device.

```python
import math
import jax
import jax.numpy as jnp
import numpy as np
from jax import lax

HEADS = 20
HDIM = 128
FRAME = 64
REACH = 1
BLOCK = 768
DOC_MOST = 768
TOKENS = 6144
FRAMES = 96
DOCS = 16


def draw_query_in(key, part):
    key = jax.random.fold_in(key, 11)
    return jnp.clip(jax.random.normal(key, (TOKENS, HEADS, HDIM), jnp.float32), -5.0, 5.0).astype(jnp.bfloat16)


def draw_key_in(key, part):
    key = jax.random.fold_in(key, 12)
    return jnp.clip(jax.random.normal(key, (TOKENS, HEADS, HDIM), jnp.float32), -5.0, 5.0).astype(jnp.bfloat16)


def plant(entries, key, least, top_value):
    dims = entries.shape
    place = [jax.random.randint(jax.random.fold_in(key, axis), (), 0, dims[axis]) for axis in range(len(dims))]
    entries = entries.at[tuple(place)].set(least)
    longest = dims.index(max(dims))
    place[longest] = (place[longest] + 1) % dims[longest]
    return entries.at[tuple(place)].set(top_value)


def block_scale(rng, shape, pieces, low, largest):
    level, own = 1.0, jax.random.fold_in(rng, 6)
    for dim, blocks in pieces:
        heights = jnp.exp(jax.random.uniform(jax.random.fold_in(own, dim), (blocks,), jnp.float32, low / len(pieces), largest / len(pieces)))
        level = level * jnp.repeat(heights, shape[dim] // blocks).reshape([-1 if axis == dim else 1 for axis in range(len(shape))])
    return level


def profile(count, total, most, skew):
    loads = [(1 << 20) // math.isqrt(standing ** skew) + 1 for standing in range(2, count + 1)]
    surplus, given = total - most - (count - 1), [1] * (count - 1)
    while surplus > 0:
        candidates = [i for i in range(count - 1) if given[i] < most]
        mass, remaining = sum([loads[i] for i in candidates]), surplus
        for i in candidates:
            addition = min(most - given[i], max(1, remaining * loads[i] // mass), surplus)
            given[i] = given[i] + addition
            surplus = surplus - addition
    return np.array([most] + given)


def ragged(rng, number_of, total, limit, lean):
    if number_of == 2:
        one = jax.random.randint(rng, (), max(1, total - limit), min(limit, total - 1) + 1)
        return jnp.stack([one, total - one])
    sizes = jnp.asarray(profile(number_of, total, limit, lean), jnp.int32)
    pairs = (number_of - 1) // 2
    giver, receiver = sizes[1:1 + 2 * pairs:2], sizes[2:2 + 2 * pairs:2]
    slack = jnp.minimum(giver - 1, limit - receiver)
    moved = jax.random.randint(jax.random.fold_in(rng, 1), (pairs,), 0, 1 << 20) % (slack + 1)
    sizes = sizes.at[1:1 + 2 * pairs:2].set(giver - moved).at[2:2 + 2 * pairs:2].set(receiver + moved)
    return sizes[jax.random.permutation(jax.random.fold_in(rng, 2), number_of)]


def noise(rng, extent, width, limit, pieces=(), kind=jnp.bfloat16):
    array = width * jax.random.normal(rng, extent, jnp.float32)
    if pieces:
        array = array * block_scale(rng, extent, pieces, -0.22, 0.18)
    return jnp.clip(array, -limit, limit).astype(kind)


def setup_inputs(seed: int = 0) -> dict:
    key_of = jax.random.split(jax.random.key(seed), 7)
    return {
        "query_in": draw_query_in(jax.random.fold_in(key_of[6], 71), 0),
        "key_in": draw_key_in(jax.random.fold_in(key_of[6], 71), 0),
        "value_in": noise(key_of[2], (TOKENS, HEADS, HDIM), 1.0, 6.0, ((0, 32),)),
        "grad_out": noise(key_of[3], (TOKENS, HEADS, HDIM), 1.0, 6.0, ((0, 32),)),
        "doc_ids": jnp.searchsorted(jnp.cumsum(ragged(key_of[4], DOCS, TOKENS, DOC_MOST, 2)), jnp.arange(TOKENS), side="right").astype(jnp.int32),
        "frame_kind": plant((jax.random.randint(key_of[5], (FRAMES,), 0, 2) < 1).astype(jnp.int32), jax.random.fold_in(key_of[5], 1), 0, 1),
    }


def reference(query_in, key_in, value_in, grad_out, doc_ids, frame_kind):
    margin = REACH * BLOCK
    window = margin + BLOCK
    head_pad = jnp.zeros((margin, HEADS, HDIM), jnp.float32)
    query_all = query_in.astype(jnp.float32)
    grad_all = grad_out.astype(jnp.float32)
    key_pad = jnp.concatenate([head_pad, key_in.astype(jnp.float32)], axis=0)
    value_pad = jnp.concatenate([head_pad, value_in.astype(jnp.float32)], axis=0)
    doc_pad = jnp.concatenate([jnp.full((margin,), -1, jnp.int32), doc_ids.astype(jnp.int32)])
    score_scale = HDIM ** -0.5
    offsets = jnp.arange(window, dtype=jnp.int32)
    local_rows = jnp.arange(BLOCK, dtype=jnp.int32)

    def one_block(carry, block_at):
        grad_keys, grad_values = carry
        query_start = block_at * BLOCK
        query = lax.dynamic_slice_in_dim(query_all, query_start, BLOCK, 0)
        grad_rows = lax.dynamic_slice_in_dim(grad_all, query_start, BLOCK, 0)
        keys_win = lax.dynamic_slice_in_dim(key_pad, query_start, window, 0)
        values_win = lax.dynamic_slice_in_dim(value_pad, query_start, window, 0)
        query_pos = query_start + local_rows
        key_pos = query_start - margin + offsets
        query_docs = lax.dynamic_slice_in_dim(doc_ids, query_start, BLOCK)
        key_docs = lax.dynamic_slice_in_dim(doc_pad, query_start, window)
        kind_table = lax.dynamic_slice_in_dim(frame_kind, query_start // FRAME, BLOCK // FRAME)
        query_kind = jnp.repeat(kind_table, FRAME)
        query_frame = query_pos // FRAME
        key_frame = key_pos // FRAME
        same_doc = query_docs[:, None] == key_docs[None, :]
        earlier = key_frame[None, :] < query_frame[:, None]
        in_frame = (key_frame[None, :] == query_frame[:, None]) & ((query_kind[:, None] == 1) | (key_pos[None, :] <= query_pos[:, None]))
        allowed = same_doc & (earlier | in_frame)
        scores = jnp.einsum("qhd,khd->hqk", query, keys_win) * score_scale
        scores = jnp.where(allowed[None], scores, -jnp.inf)
        row_max = jnp.max(scores, axis=2, keepdims=True)
        raised = jnp.exp(scores - row_max)
        prob_rows = raised / jnp.sum(raised, axis=2, keepdims=True)
        weights = lax.optimization_barrier(prob_rows.astype(jnp.bfloat16)).astype(jnp.float32)
        output = jnp.einsum("hqk,khd->qhd", weights, values_win).astype(jnp.bfloat16)
        row_delta = jnp.einsum("qhd,qhd->hq", grad_rows, output.astype(jnp.float32))
        grad_prob = jnp.einsum("qhd,khd->hqk", grad_rows, values_win)
        grad_score = lax.optimization_barrier((prob_rows * (grad_prob - row_delta[:, :, None])).astype(jnp.bfloat16)).astype(jnp.float32)
        grad_query = (jnp.einsum("hqk,khd->qhd", grad_score, keys_win) * score_scale).astype(jnp.bfloat16)
        key_term = jnp.einsum("hqk,qhd->khd", grad_score, query) * score_scale
        value_term = jnp.einsum("hqk,qhd->khd", weights, grad_rows)
        grad_keys = lax.dynamic_update_slice_in_dim(grad_keys, lax.dynamic_slice_in_dim(grad_keys, query_start, window, 0) + key_term, query_start, 0)
        grad_values = lax.dynamic_update_slice_in_dim(grad_values, lax.dynamic_slice_in_dim(grad_values, query_start, window, 0) + value_term, query_start, 0)
        return (grad_keys, grad_values), (output, grad_query)

    zero_pad = jnp.zeros((TOKENS + margin, HEADS, HDIM), jnp.float32)
    carried, stacked = lax.scan(one_block, (zero_pad, zero_pad), jnp.arange(TOKENS // BLOCK, dtype=jnp.int32))
    grad_keys, grad_values = carried
    outputs, grad_queries = stacked
    return (outputs.reshape(TOKENS, HEADS, HDIM), grad_queries.reshape(TOKENS, HEADS, HDIM), grad_keys[margin:].astype(jnp.bfloat16), grad_values[margin:].astype(jnp.bfloat16))
```

```python
import functools
import math

import jax
import jax.numpy as jnp
from jax import lax
from jax.experimental import pallas as pl
from jax.experimental.pallas import tpu as pltpu
from jax.sharding import PartitionSpec as P

FRAME = 64
REACH = 1
AXES = ("ctx", "head")
GROUP = 4
MASKED = -1e30
CHUNKS = (2, 2, 2, 2, 2)
INFLIGHT = 2


def dot(a, b, dims):
    return lax.dot_general(a, b, (dims, ((), ())), preferred_element_type=jnp.float32)


NT = ((1,), (1,))
TN = ((0,), (0,))
NN = ((1,), (0,))


def forward_kernel(q_ref, kv0_ref, kv1_ref, kv2_ref, rows_ref, cols_ref, out_ref, stat_ref, *, scale):
    span = q_ref.shape[2]
    factor = scale * math.log2(math.e)
    cuts = (0, 256, span) if span > 256 else (0, span)
    for a, b in zip(cuts[:-1], cuts[1:]):
        query = q_ref[0, 0, a:b, :]
        grad = q_ref[1, 0, a:b, :]
        doc_row = rows_ref[0:1, a:b]
        limit_row = rows_ref[1:2, a:b]
        segments = ((kv2_ref, a, span, 0), (kv1_ref, 0, span, span), (kv0_ref, 0, b, 2 * span))
        scores = []
        for ref, lo, hi, offset in segments:
            raw = dot(ref[0, 0, lo:hi, :], query, NT) * factor
            key_doc = cols_ref[offset + lo : offset + hi, :]
            allowed = key_doc == doc_row
            if ref is kv0_ref:
                place = lo + lax.broadcasted_iota(jnp.int32, raw.shape, 0)
                allowed = allowed & (place <= limit_row)
            scores.append(jnp.where(allowed, raw, MASKED))
        top = functools.reduce(jnp.maximum, [jnp.max(s, axis=0, keepdims=True) for s in scores])
        raised = [jnp.exp2(s - top) for s in scores]
        total = functools.reduce(jnp.add, [jnp.sum(r, axis=0, keepdims=True) for r in raised])
        inverse = 1.0 / total
        probs = [r * inverse for r in raised]
        mixed = functools.reduce(
            jnp.add,
            [
                dot(ref[1, 0, lo:hi, :], p.astype(jnp.bfloat16), TN)
                for (ref, lo, hi, _), p in zip(segments, probs)
            ],
        )
        output = mixed.astype(jnp.bfloat16)
        grad_t = grad.astype(jnp.float32).T
        delta = jnp.sum(grad_t * output.astype(jnp.float32), axis=0, keepdims=True)
        grad_query = jnp.zeros_like(mixed)
        for (ref, lo, hi, _), p in zip(segments, probs):
            grad_prob = dot(ref[1, 0, lo:hi, :], grad, NT)
            grad_score = (p * (grad_prob - delta)).astype(jnp.bfloat16)
            grad_query += dot(ref[0, 0, lo:hi, :], grad_score, TN)
        out_ref[0, 0, a:b, :] = mixed.T.astype(jnp.bfloat16)
        out_ref[1, 0, a:b, :] = (grad_query * scale).T.astype(jnp.bfloat16)
        stat_ref[0, 0:1, a:b] = top + jnp.log2(total)
        stat_ref[0, 1:2, a:b] = delta


def backward_kernel(kv_ref, q0_ref, q1_ref, q2_ref, st0_ref, st1_ref, st2_ref, rows_ref, cols_ref, out_ref, *, scale):
    span = kv_ref.shape[2]
    factor = scale * math.log2(math.e)
    for a in range(0, span, 128):
        b = a + 128
        key = kv_ref[0, 0, a:b, :]
        value = kv_ref[1, 0, a:b, :]
        key_doc = cols_ref[a:b, :]
        grad_key = jnp.zeros((b - a, key.shape[1]), jnp.float32)
        grad_value = jnp.zeros((b - a, key.shape[1]), jnp.float32)
        segments = (
            (q0_ref, st0_ref, a, span, 0),
            (q1_ref, st1_ref, 0, span, span),
            (q2_ref, st2_ref, 0, b, 2 * span),
        )
        for ref, stats, lo, hi, offset in segments:
            query = ref[0, 0, lo:hi, :]
            grad = ref[1, 0, lo:hi, :]
            raw = dot(key, query, NT) * factor
            allowed = key_doc == rows_ref[0:1, offset + lo : offset + hi]
            if ref is q0_ref:
                place = a + lax.broadcasted_iota(jnp.int32, raw.shape, 0)
                allowed = allowed & (place <= rows_ref[1:2, lo:hi])
            probs = jnp.exp2(jnp.where(allowed, raw - stats[0, 0:1, lo:hi], MASKED))
            grad_value += dot(probs.astype(jnp.bfloat16), grad, NN)
            grad_prob = dot(value, grad, NT)
            grad_score = (probs * (grad_prob - stats[0, 1:2, lo:hi])).astype(jnp.bfloat16)
            grad_key += dot(grad_score, query, NN)
        out_ref[0, 0, a:b, :] = (grad_key * scale).astype(jnp.bfloat16)
        out_ref[1, 0, a:b, :] = grad_value.astype(jnp.bfloat16)


def per_head(shape):
    return pl.BlockSpec((shape[0], 1) + shape[2:], lambda h: (0, h, 0, 0))


def per_head_stats(shape):
    return pl.BlockSpec((1,) + shape[1:], lambda h: (h, 0, 0))


def whole(shape):
    return pl.BlockSpec(shape, lambda h: (0,) * len(shape))


def cost(heads, span, dim, matmuls):
    pairs = heads * span * span * 3
    return pl.CostEstimate(
        flops=2 * pairs * dim * matmuls, bytes_accessed=heads * span * dim * 2 * 10, transcendentals=pairs
    )


def attend_forward(q, kv0, kv1, kv2, rows, cols, scale):
    _, heads, span, dim = q.shape
    return pl.pallas_call(
        functools.partial(forward_kernel, scale=scale),
        grid=(heads,),
        in_specs=[per_head(q.shape)] * 4 + [whole(rows.shape), whole(cols.shape)],
        out_specs=[per_head(q.shape), per_head_stats((heads, 2, span))],
        out_shape=[
            jax.ShapeDtypeStruct(q.shape, jnp.bfloat16),
            jax.ShapeDtypeStruct((heads, 2, span), jnp.float32),
        ],
        compiler_params=pltpu.CompilerParams(vmem_limit_bytes=40 * 2**20),
        cost_estimate=cost(heads, span, dim, 4),
    )(q, kv0, kv1, kv2, rows, cols)


def attend_backward(kv, q0, q1, q2, st0, st1, st2, rows, cols, scale):
    _, heads, span, dim = kv.shape
    return pl.pallas_call(
        functools.partial(backward_kernel, scale=scale),
        grid=(heads,),
        in_specs=[per_head(kv.shape)] * 4
        + [per_head_stats(st0.shape)] * 3
        + [whole(rows.shape), whole(cols.shape)],
        out_specs=per_head(kv.shape),
        out_shape=jax.ShapeDtypeStruct(kv.shape, jnp.bfloat16),
        compiler_params=pltpu.CompilerParams(vmem_limit_bytes=40 * 2**20),
        cost_estimate=cost(heads, span, dim, 4),
    )(kv, q0, q1, q2, st0, st1, st2, rows, cols)


def tied(x, *after):
    return lax.optimization_barrier((x,) + after)[0] if after else x


def local(query_in, key_in, value_in, grad_out, doc_ids, frame_kind):
    rows_own, heads, dim = query_in.shape
    half = heads // 2
    span = 2 * rows_own
    count = lax.axis_size("ctx") * lax.axis_size("head")
    at = lax.axis_index("ctx") * lax.axis_size("head") + lax.axis_index("head")
    core = at % 2
    side = (at // 2) % 2
    base = (at - core) * rows_own
    scale = dim**-0.5

    def shifted(x, by):
        return lax.ppermute(x, AXES, [(i, i + by) for i in range(count) if 0 <= i + by < count])

    def swapped(x, bit):
        return lax.ppermute(x, AXES, [(i, i ^ bit) for i in range(count)])

    reach = 2 * span
    docs = jnp.concatenate(
        [jnp.full((reach,), -1, jnp.int32), doc_ids, jnp.full((reach,), -2, jnp.int32)]
    )
    docs = lax.dynamic_slice_in_dim(docs, base, 5 * span)
    kinds = jnp.concatenate([frame_kind, jnp.zeros((reach // FRAME,), jnp.int32)])
    kinds = lax.dynamic_slice_in_dim(kinds, base // FRAME, 3 * span // FRAME)
    place = jnp.arange(3 * span, dtype=jnp.int32)
    limit = jnp.where(jnp.repeat(kinds, FRAME) == 1, (place // FRAME) * FRAME + FRAME - 1, place)
    rows = jnp.stack([docs[reach:], limit])
    cols = docs[: 3 * span, None]

    def halves(x, y, which):
        pick = lambda a: lax.dynamic_slice_in_dim(a.transpose(1, 0, 2), which * half, half, 0)
        return jnp.stack([pick(x), pick(y)])

    def pieces(x, y):
        own = halves(x, y, core)
        came = swapped(halves(x, y, 1 - core), 1)
        out, start = [], 0
        for size in CHUNKS:
            a, b = own[:, start : start + size], came[:, start : start + size]
            first, second = jnp.where(core == 0, a, b), jnp.where(core == 0, b, a)
            out.append(jnp.concatenate([first, second], axis=2))
            start += size
        return out

    kv0 = pieces(key_in, value_in)
    q0 = pieces(query_in, grad_out)
    n = len(CHUNKS)
    far, near = [], []
    for j in range(2 * n):
        mine = kv0[j] if j < n else q0[j - n]
        after = [far[j - INFLIGHT]] if j >= INFLIGHT else []
        far.append(shifted(tied(mine, *after), GROUP if j < n else -GROUP))
    for j in range(2 * n):
        if j < n:
            sent = jnp.where(side == 0, kv0[j], far[j])
        else:
            sent = jnp.where(side == 0, far[j], q0[j - n])
        after = [near[j - INFLIGHT]] if j >= INFLIGHT else []
        near.append(swapped(tied(sent, *after), 2))

    forward = [
        attend_forward(q0[j], kv0[j], near[j], far[j], rows[:, :span], cols, scale) for j in range(n)
    ]
    st0 = jnp.concatenate([f[1] for f in forward], axis=0)
    st2 = shifted(st0, -GROUP)
    st1 = swapped(jnp.where(side == 0, st2, st0), 2)
    own_cols = cols[2 * span :]
    outs, start = [], 0
    for j, size in enumerate(CHUNKS):
        cut = slice(start, start + size)
        outs.append(
            attend_backward(
                kv0[j], q0[j], near[n + j], far[n + j], st0[cut], st1[cut], st2[cut], rows, own_cols, scale
            )
        )
        start += size

    def returned(parts):
        keep, back = [], []
        for part in parts:
            low, high = part[:, :, :rows_own], part[:, :, rows_own:]
            keep.append(jnp.where(core == 0, low, high))
            back.append(swapped(jnp.where(core == 0, high, low), 1))
        keep = jnp.concatenate(keep, axis=1)
        back = jnp.concatenate(back, axis=1)
        both = jnp.concatenate([jnp.where(core == 0, keep, back), jnp.where(core == 0, back, keep)], axis=1)
        return both[0].transpose(1, 0, 2), both[1].transpose(1, 0, 2)

    output, grad_query = returned([jnp.concatenate([f[0] for f in forward], axis=1)])
    grad_key, grad_value = returned(outs)
    return output, grad_query, grad_key, grad_value


def solution(mesh):
    placed = P(AXES, None, None)
    return jax.shard_map(
        local,
        mesh=mesh,
        in_specs=(placed,) * 4 + (P(), P()),
        out_specs=(placed,) * 4,
        check_vma=False,
    )
```

```python
import functools
import math

import jax
import jax.numpy as jnp
from jax import lax
from jax.experimental import pallas as pl
from jax.experimental.pallas import tpu as pltpu
from jax.sharding import PartitionSpec as P

FRAME = 64
AXES = ("ctx", "head")
GROUP = 4
MASKED = -1e30
KEY_CHUNKS = (3, 4, 3)
QUERY_CHUNKS = (4, 3, 2, 1)
FAR_IN_FLIGHT = 2
NEAR_IN_FLIGHT = 2
FORWARD_LEAD = 3
BACKWARD_LEAD = 3
OUTPUT_LEAD = 2
QUERY_TIE = 3
KERNEL_LAG = 0
COST = 1.0
VMEM = 16 * 2**20
SMALL = 8 * 2**20
NT = ((1,), (1,))
NN = ((1,), (0,))


def dot(a, b, dims):
    return lax.dot_general(a, b, (dims, ((), ())), preferred_element_type=jnp.float32)


def starts(sizes):
    return [sum(sizes[:i]) for i in range(len(sizes))]


def by_core(scratch, keep_ref, send_ref, core):
    rows = keep_ref.shape[2]
    mine = pl.multiple_of(core * rows, rows)
    other = pl.multiple_of((1 - core) * rows, rows)
    keep_ref[:, 0] = scratch[:, pl.ds(mine, rows), :]
    send_ref[:, 0] = scratch[:, pl.ds(other, rows), :]


def forward_kernel(
    where_ref, q_ref, kv0_ref, kv1_ref, kv2_ref, near_ref, docs_ref, keep_ref, send_ref, stat_ref, done, *, scale
):
    span = q_ref.shape[2]
    factor = scale * math.log2(math.e)
    core = where_ref[1]
    query, grad = q_ref[0, 0], q_ref[1, 0]
    doc_col, limit_col = near_ref[:, 0:1], near_ref[:, 1:2]
    segments = ((kv2_ref[0, 0], kv2_ref[1, 0]), (kv1_ref[0, 0], kv1_ref[1, 0]), (kv0_ref[0, 0], kv0_ref[1, 0]))
    scores = []
    for i, (key, _) in enumerate(segments):
        raw = dot(query, key, NT) * factor
        allowed = docs_ref[:, i * span : (i + 1) * span] == doc_col
        if i == 2:
            place = lax.broadcasted_iota(jnp.int32, raw.shape, 1)
            allowed = allowed & (place <= limit_col)
        scores.append(jnp.where(allowed, raw, MASKED))
    top = functools.reduce(jnp.maximum, [jnp.max(s, axis=1, keepdims=True) for s in scores])
    raised = [jnp.exp2(s - top) for s in scores]
    total = functools.reduce(jnp.add, [jnp.sum(r, axis=1, keepdims=True) for r in raised])
    inverse = 1.0 / total
    probs = [r * inverse for r in raised]
    mixed = functools.reduce(
        jnp.add, [dot(p.astype(jnp.bfloat16), value, NN) for (_, value), p in zip(segments, probs)]
    )
    output = mixed.astype(jnp.bfloat16)
    delta = jnp.sum(grad.astype(jnp.float32) * output.astype(jnp.float32), axis=1, keepdims=True)
    grad_query = jnp.zeros_like(mixed)
    for (key, value), p in zip(segments, probs):
        grad_score = (p * (dot(grad, value, NT) - delta)).astype(jnp.bfloat16)
        grad_query += dot(grad_score, key, NN)
    done[0] = output
    done[1] = (grad_query * scale).astype(jnp.bfloat16)
    for i, column in enumerate((top + jnp.log2(total), delta)):
        stat_ref[0, i : i + 1, :] = jnp.broadcast_to(column, (span, 128)).T[0:1]
    by_core(done, keep_ref, send_ref, core)


def backward_kernel(
    where_ref, kv_ref, q0_ref, q1_ref, q2_ref, st0_ref, st1_ref, st2_ref, rows_ref, near_ref, keep_ref, send_ref, done, *, scale
):
    span = kv_ref.shape[2]
    factor = scale * math.log2(math.e)
    core = where_ref[1]
    key, value = kv_ref[0, 0], kv_ref[1, 0]
    key_doc = near_ref[:, 0:1]
    grad_key = jnp.zeros(key.shape, jnp.float32)
    grad_value = jnp.zeros(key.shape, jnp.float32)
    segments = (
        (q0_ref[0, 0], q0_ref[1, 0], st0_ref),
        (q1_ref[0, 0], q1_ref[1, 0], st1_ref),
        (q2_ref[0, 0], q2_ref[1, 0], st2_ref),
    )
    for i, (query, grad, stats) in enumerate(segments):
        raw = dot(key, query, NT) * factor
        allowed = key_doc == rows_ref[0:1, i * span : (i + 1) * span]
        if i == 0:
            place = lax.broadcasted_iota(jnp.int32, raw.shape, 0)
            allowed = allowed & (place <= rows_ref[1:2, :span])
        probs = jnp.exp2(jnp.where(allowed, raw - stats[0, 0:1], MASKED))
        grad_value += dot(probs.astype(jnp.bfloat16), grad, NN)
        grad_prob = dot(value, grad, NT)
        grad_score = (probs * (grad_prob - stats[0, 1:2])).astype(jnp.bfloat16)
        grad_key += dot(grad_score, query, NN)
    done[0] = (grad_key * scale).astype(jnp.bfloat16)
    done[1] = grad_value.astype(jnp.bfloat16)
    by_core(done, keep_ref, send_ref, core)


def per_head(shape, start=0):
    return pl.BlockSpec((shape[0], 1) + shape[2:], lambda h: (0, h + start, 0, 0))


def per_head_stats(shape, start=0):
    return pl.BlockSpec((1,) + shape[1:], lambda h: (h + start, 0, 0))


def whole(shape):
    return pl.BlockSpec(shape, lambda h: (0,) * len(shape))


def cost(heads, span, dim):
    pairs = heads * span * span * 3
    return pl.CostEstimate(
        flops=int(COST * 2 * pairs * dim * 4), bytes_accessed=int(COST * heads * span * dim * 2 * 10), transcendentals=int(COST * pairs)
    )


def attend(kernel, heads, here, arrays, stats, tables, scale, gives_stats):
    _, _, span, dim = arrays[0][0].shape
    shape = (2, heads, span // 2, dim)
    out_specs = [per_head(shape), per_head(shape)]
    out_shape = [jax.ShapeDtypeStruct(shape, jnp.bfloat16)] * 2
    if gives_stats:
        out_specs.append(per_head_stats((heads, 2, span)))
        out_shape.append(jax.ShapeDtypeStruct((heads, 2, span), jnp.float32))
    return pl.pallas_call(
        functools.partial(kernel, scale=scale),
        grid=(heads,),
        in_specs=[pl.BlockSpec(memory_space=pltpu.SMEM)]
        + [per_head(x.shape, first) for x, first in arrays]
        + [per_head_stats(x.shape, first) for x, first in stats]
        + [whole(x.shape) for x in tables],
        out_specs=out_specs,
        out_shape=out_shape,
        scratch_shapes=[pltpu.VMEM((2, span, dim), jnp.bfloat16)],
        compiler_params=pltpu.CompilerParams(vmem_limit_bytes=VMEM),
        cost_estimate=cost(heads, span, dim),
    )(here, *[x for x, _ in arrays], *[x for x, _ in stats], *tables)


def finish(copies, sems):
    running = [pltpu.make_async_copy(a, b, sems.at[i]) for i, (a, b) in enumerate(copies)]
    for c in running:
        c.start()
    for c in running:
        c.wait()


def laid_out(where_ref, x_ref, y_ref, came_ref, *rest, cuts):
    parts, staged, sems = rest[:-2], rest[-2], rest[-1]
    core = where_ref[1]
    half, rows = came_ref.shape[1], came_ref.shape[2]
    mine = pl.multiple_of(core * rows, rows)
    other = pl.multiple_of((1 - core) * rows, rows)
    own = pl.ds(core * half, half)
    finish(
        [
            (x_ref.at[own], staged.at[0, :, pl.ds(mine, rows)]),
            (y_ref.at[own], staged.at[1, :, pl.ds(mine, rows)]),
            (came_ref, staged.at[:, :, pl.ds(other, rows)]),
        ],
        sems,
    )
    finish([(staged.at[:, pl.ds(at, size)], part) for part, (at, size) in zip(parts, cuts)], sems)


def lay_out(here, x, y, came, cuts):
    half, rows, dim = came.shape[1:]
    return pl.pallas_call(
        functools.partial(laid_out, cuts=cuts),
        in_specs=[pl.BlockSpec(memory_space=pltpu.SMEM)]
        + [pl.BlockSpec(memory_space=pltpu.HBM)] * 2
        + [pl.BlockSpec(memory_space=pl.ANY)],
        out_specs=[pl.BlockSpec(memory_space=pl.ANY)] * len(cuts),
        out_shape=[jax.ShapeDtypeStruct((2, n, 2 * rows, dim), x.dtype) for _, n in cuts],
        scratch_shapes=[pltpu.VMEM((2, half, 2 * rows, dim), x.dtype), pltpu.SemaphoreType.DMA((3 + len(cuts),))],
        compiler_params=pltpu.CompilerParams(vmem_limit_bytes=SMALL),
        cost_estimate=pl.CostEstimate(flops=0, bytes_accessed=8 * half * rows * dim * 2, transcendentals=0),
    )(here, x, y, came)


def gathered(where_ref, *refs, sizes):
    n = len(sizes)
    kept, came, results, sems = refs[:n], refs[n : 2 * n], refs[2 * n : 2 * n + 2], refs[-1]
    core = where_ref[1]
    half = sum(sizes)
    copies = []
    for j, (begin, size) in enumerate(zip(starts(sizes), sizes)):
        for i, to in enumerate(results):
            copies.append((kept[j].at[i], to.at[pl.ds(core * half + begin, size)]))
            copies.append((came[j].at[i], to.at[pl.ds((1 - core) * half + begin, size)]))
    finish(copies, sems)


def gather(here, kept, came):
    sizes = tuple(k.shape[1] for k in kept)
    _, _, rows, dim = kept[0].shape
    shape = (2 * sum(sizes), rows, dim)
    return pl.pallas_call(
        functools.partial(gathered, sizes=sizes),
        in_specs=[pl.BlockSpec(memory_space=pltpu.SMEM)] + [pl.BlockSpec(memory_space=pltpu.VMEM)] * (2 * len(sizes)),
        out_specs=[pl.BlockSpec(memory_space=pltpu.HBM)] * 2,
        out_shape=[jax.ShapeDtypeStruct(shape, kept[0].dtype)] * 2,
        scratch_shapes=[pltpu.SemaphoreType.DMA((4 * len(sizes),))],
        compiler_params=pltpu.CompilerParams(vmem_limit_bytes=SMALL),
        cost_estimate=pl.CostEstimate(flops=0, bytes_accessed=8 * sum(sizes) * rows * dim * 2, transcendentals=0),
    )(here, *kept, *came)


def tied(x, *after):
    return lax.optimization_barrier((x,) + after)[0] if after else x


def local(query_in, key_in, value_in, grad_out, doc_ids, frame_kind):
    rows_own, heads, dim = query_in.shape
    half = heads // 2
    span = 2 * rows_own
    count = lax.axis_size("ctx") * lax.axis_size("head")
    at = lax.axis_index("ctx") * lax.axis_size("head") + lax.axis_index("head")
    core = at % 2
    side = (at // 2) % 2
    base = (at - core) * rows_own
    scale = dim**-0.5
    here = jnp.stack([side, core]).astype(jnp.int32)

    def sent(x, pairs, name):
        with jax.named_scope(name):
            return lax.ppermute(x, AXES, [(i, j) for i, j in pairs if 0 <= j < count])

    ahead = [(i, i + GROUP) for i in range(count)]
    behind = [(i, i - GROUP) for i in range(count)]
    across = [(i, i ^ 1) for i in range(count)]
    beside = [(i, i ^ 2) for i in range(count)]
    before = [(i, i - 2) for i in range(count)]

    by_head = [x.transpose(1, 0, 2) for x in (key_in, value_in, query_in, grad_out)]

    def theirs(x, y):
        return jnp.stack([lax.dynamic_slice_in_dim(a, (1 - core) * half, half, 0) for a in (x, y)])

    key_cuts = tuple(zip(starts(KEY_CHUNKS), KEY_CHUNKS))
    query_cuts = tuple(zip(starts(QUERY_CHUNKS), QUERY_CHUNKS))
    edges = sorted({a for a, _ in key_cuts + query_cuts}) + [half]
    calls = tuple((a, b - a) for a, b in zip(edges[:-1], edges[1:]))
    nk, nq = len(KEY_CHUNKS), len(QUERY_CHUNKS)
    came_kv = sent(theirs(*by_head[:2]), across, "pair_kv")
    kv_parts = lay_out(here, *by_head[:2], came_kv, key_cuts)
    came_q = sent(tied(theirs(*by_head[2:]), came_kv), across, "pair_q")
    q_parts = lay_out(here, *by_head[2:], came_q, query_cuts)

    doc_ids, frame_kind = tied((doc_ids, frame_kind), came_q)
    reach = 2 * span
    docs = jnp.concatenate(
        [jnp.full((reach,), -1, jnp.int32), doc_ids, jnp.full((reach,), -2, jnp.int32)]
    )
    docs = lax.dynamic_slice_in_dim(docs, base, 5 * span)
    kinds = jnp.concatenate([frame_kind, jnp.zeros((reach // FRAME,), jnp.int32)])
    kinds = lax.dynamic_slice_in_dim(kinds, base // FRAME, 3 * span // FRAME)
    place = jnp.arange(3 * span, dtype=jnp.int32)
    limit = jnp.where(jnp.repeat(kinds, FRAME) == 1, (place // FRAME) * FRAME + FRAME - 1, place)
    rows = jnp.stack([docs[reach:], limit])
    near_docs = rows[:, :span].T
    key_docs = docs[None, : 3 * span]

    def part(parts, cuts, start):
        k = max(i for i, (first, _) in enumerate(cuts) if first <= start)
        return parts[k], start - cuts[k][0]

    def ready(cuts, count):
        have = sum(size for _, size in cuts[:count])
        return [i for i, (start, size) in enumerate(calls) if start + size <= have]

    far = []
    for j, piece in enumerate(kv_parts + q_parts):
        after = [far[j - FAR_IN_FLIGHT]] if j >= FAR_IN_FLIGHT else []
        if j == QUERY_TIE and 0 < j < nk:
            after.append(q_parts[0])
        far.append(sent(tied(piece, *after), ahead if j < nk else behind, f"far_{j}"))
    near, forward, backward, results, kept = [], [], [], [], []
    for j, piece in enumerate(kv_parts + q_parts):
        first, second = (piece, far[j]) if j < nk else (far[j], piece)
        after = [near[j - NEAR_IN_FLIGHT]] if j >= NEAR_IN_FLIGHT else []
        if FORWARD_LEAD:
            after += [forward[i][0] for i in ready(key_cuts, max(0, j + 1 - FORWARD_LEAD))]
        if BACKWARD_LEAD:
            after += [backward[i][0] for i in ready(query_cuts, max(0, j + 1 - nk - BACKWARD_LEAD))]
        if OUTPUT_LEAD and j >= nk + nq - OUTPUT_LEAD:
            after += results
        near.append(sent(tied(jnp.where(side == 0, first, second), *after), beside, f"near_{j}"))
        for i in ready(key_cuts, min(j + 1, nk))[len(forward) :]:
            start, size = calls[i]
            arrays = [part(q_parts, query_cuts, start)]
            arrays += [part(x, key_cuts, start) for x in (kv_parts, near, far)]
            if KERNEL_LAG:
                x, at_head = arrays[2]
                arrays[2] = (tied(x, far[min(j + KERNEL_LAG, nk + nq - 1)]), at_head)
            forward.append(attend(forward_kernel, size, here, arrays, [], [near_docs, key_docs], scale, True))
        if len(forward) == len(calls) and not kept:
            st0 = jnp.concatenate([f[2] for f in forward], axis=0)
            kept = [st0, sent(st0, before, "next_stats"), sent(st0, behind, "far_stats")]
            results = gather(here, [p[0] for p in forward], [sent(p[1], across, "pair_out") for p in forward])
        if j >= nk:
            for i in ready(query_cuts, j + 1 - nk)[len(backward) :]:
                start, size = calls[i]
                arrays = [part(kv_parts, key_cuts, start)]
                arrays += [part(x, query_cuts, start) for x in (q_parts, near[nk:], far[nk:])]
                if KERNEL_LAG:
                    x, at_head = arrays[2]
                    arrays[2] = (tied(x, far[min(j + KERNEL_LAG, nk + nq - 1)]), at_head)
                stats = [(x, start) for x in kept]
                backward.append(attend(backward_kernel, size, here, arrays, stats, [rows, near_docs], scale, False))

    results = list(results) + list(
        gather(here, [p[0] for p in backward], [sent(p[1], across, "pair_out") for p in backward])
    )
    return tuple(x.transpose(1, 0, 2) for x in results)


def solution(mesh):
    placed = P(AXES, None, None)
    return jax.shard_map(
        local,
        mesh=mesh,
        in_specs=(placed,) * 4 + (P(), P()),
        out_specs=(placed,) * 4,
        check_vma=False,
    )
```

```python
import functools
import math

import jax
import jax.numpy as jnp
from jax import lax
from jax.experimental import pallas as pl
from jax.experimental.pallas import tpu as pltpu
from jax.sharding import PartitionSpec as P

FRAME = 64
AXES = ("ctx", "head")
GROUP = 4
MASKED = -1e30
CHUNKS = (2, 2, 1)
COST = 0.1
GATHER_BEFORE = 2
OVERLAP = True
VMEM = 16 * 2**20
SMALL = 8 * 2**20
NT = ((1,), (1,))
NN = ((1,), (0,))


def dot(a, b, dims):
    return lax.dot_general(a, b, (dims, ((), ())), preferred_element_type=jnp.float32)


def starts(sizes):
    return [sum(sizes[:i]) for i in range(len(sizes))]


def placed(done, side, core, keep_ref, theirs_ref, send_ref):
    rows = keep_ref.shape[2]
    mine = pl.multiple_of(core * rows, rows)
    other = pl.multiple_of((1 - core) * rows, rows)
    keep_ref[:, 0] = done[side, :, pl.ds(mine, rows), :]
    theirs_ref[:, 0] = done[side, :, pl.ds(other, rows), :]
    send_ref[:, 0] = done[1 - side]


def ordered(side, own_ref, beside_ref):
    first, second = [], []
    for i in range(2):
        own, beside = own_ref[i, 0], beside_ref[i, 0]
        first.append(jnp.where(side == 0, own, beside))
        second.append(jnp.where(side == 0, beside, own))
    return [tuple(first), tuple(second)]


def forward_kernel(
    where_ref, q_own, q_beside, kv_own, kv_beside, past_own, past_beside, cols_ref, docs_ref,
    keep_ref, theirs_ref, send_ref, stat_ref, done, *, scale
):
    span = q_own.shape[2]
    factor = scale * math.log2(math.e)
    side, core = where_ref[0], where_ref[1]
    queries = ordered(side, q_own, q_beside)
    blocks = ordered(side, past_own, past_beside) + ordered(side, kv_own, kv_beside)
    for part in range(2):
        query, grad = queries[part]
        at = part * span
        doc_col, limit_col = cols_ref[at : at + span, 0:1], cols_ref[at : at + span, 1:2]
        segments = blocks[part : part + 3]
        scores = []
        for i, (key, _) in enumerate(segments):
            raw = dot(query, key, NT) * factor
            allowed = docs_ref[:, at + i * span : at + (i + 1) * span] == doc_col
            if i == 2:
                place = at + lax.broadcasted_iota(jnp.int32, raw.shape, 1)
                allowed = allowed & (place <= limit_col)
            scores.append(jnp.where(allowed, raw, MASKED))
        top = functools.reduce(jnp.maximum, [jnp.max(s, axis=1, keepdims=True) for s in scores])
        raised = [jnp.exp2(s - top) for s in scores]
        total = functools.reduce(jnp.add, [jnp.sum(r, axis=1, keepdims=True) for r in raised])
        inverse = 1.0 / total
        probs = [r * inverse for r in raised]
        mixed = functools.reduce(
            jnp.add, [dot(p.astype(jnp.bfloat16), value, NN) for (_, value), p in zip(segments, probs)]
        )
        output = mixed.astype(jnp.bfloat16)
        delta = jnp.sum(grad.astype(jnp.float32) * output.astype(jnp.float32), axis=1, keepdims=True)
        grad_query = jnp.zeros_like(mixed)
        for (key, value), p in zip(segments, probs):
            grad_score = (p * (dot(grad, value, NT) - delta)).astype(jnp.bfloat16)
            grad_query += dot(grad_score, key, NN)
        done[part, 0] = output
        done[part, 1] = (grad_query * scale).astype(jnp.bfloat16)
        for i, column in enumerate((top + jnp.log2(total), delta)):
            stat_ref[0, i : i + 1, at : at + span] = jnp.broadcast_to(column, (span, 128)).T[0:1]
    placed(done, side, core, keep_ref, theirs_ref, send_ref)


def backward_kernel(
    where_ref, kv_own, kv_beside, q_own, q_beside, next_own, next_beside, stat_ref, next_stat_ref, cols_ref, rows_ref,
    keep_ref, theirs_ref, send_ref, done, *, scale
):
    span = kv_own.shape[2]
    factor = scale * math.log2(math.e)
    side, core = where_ref[0], where_ref[1]
    keys = ordered(side, kv_own, kv_beside)
    blocks = ordered(side, q_own, q_beside) + ordered(side, next_own, next_beside)
    for part in range(2):
        key, value = keys[part]
        at = part * span
        key_doc = cols_ref[at : at + span, 0:1]
        grad_key = jnp.zeros(key.shape, jnp.float32)
        grad_value = jnp.zeros(key.shape, jnp.float32)
        for i in range(3):
            query, grad = blocks[part + i]
            block = part + i
            lo = block * span
            stats = stat_ref if block < 2 else next_stat_ref
            here = (block % 2) * span
            raw = dot(key, query, NT) * factor
            allowed = key_doc == rows_ref[0:1, lo : lo + span]
            if i == 0:
                place = at + lax.broadcasted_iota(jnp.int32, raw.shape, 0)
                allowed = allowed & (place <= rows_ref[1:2, lo : lo + span])
            probs = jnp.exp2(jnp.where(allowed, raw - stats[0, 0:1, here : here + span], MASKED))
            grad_value += dot(probs.astype(jnp.bfloat16), grad, NN)
            grad_prob = dot(value, grad, NT)
            grad_score = (probs * (grad_prob - stats[0, 1:2, here : here + span])).astype(jnp.bfloat16)
            grad_key += dot(grad_score, query, NN)
        done[part, 0] = (grad_key * scale).astype(jnp.bfloat16)
        done[part, 1] = grad_value.astype(jnp.bfloat16)
    placed(done, side, core, keep_ref, theirs_ref, send_ref)


def per_head(shape, start=0):
    return pl.BlockSpec((shape[0], 1) + shape[2:], lambda h: (0, h + start, 0, 0))


def per_head_stats(shape, start=0):
    return pl.BlockSpec((1,) + shape[1:], lambda h: (h + start, 0, 0))


def whole(shape):
    return pl.BlockSpec(shape, lambda h: (0,) * len(shape))


def cost(heads, span, dim):
    pairs = heads * span * span * 3
    return pl.CostEstimate(
        flops=int(COST * 2 * pairs * dim * 4), bytes_accessed=int(COST * heads * span * dim * 2 * 10), transcendentals=int(COST * pairs)
    )


def attend(kernel, heads, here, arrays, stats, tables, scale, gives_stats):
    _, _, span, dim = arrays[0][0].shape
    rows = span // 2
    shapes = [(2, heads, rows, dim), (2, heads, rows, dim), (2, heads, span, dim)]
    out_specs = [per_head(shape) for shape in shapes]
    out_shape = [jax.ShapeDtypeStruct(shape, jnp.bfloat16) for shape in shapes]
    if gives_stats:
        out_specs.append(per_head_stats((heads, 2, 2 * span)))
        out_shape.append(jax.ShapeDtypeStruct((heads, 2, 2 * span), jnp.float32))
    return pl.pallas_call(
        functools.partial(kernel, scale=scale),
        grid=(heads,),
        in_specs=[pl.BlockSpec(memory_space=pltpu.SMEM)]
        + [per_head(x.shape, first) for x, first in arrays]
        + [per_head_stats(x.shape, first) for x, first in stats]
        + [whole(x.shape) for x in tables],
        out_specs=out_specs,
        out_shape=out_shape,
        scratch_shapes=[pltpu.VMEM((2, 2, span, dim), jnp.bfloat16)],
        compiler_params=pltpu.CompilerParams(vmem_limit_bytes=VMEM),
        cost_estimate=cost(2 * heads, span, dim),
    )(here, *[x for x, _ in arrays], *[x for x, _ in stats], *tables)


def finish(copies, sems):
    running = [pltpu.make_async_copy(a, b, sems.at[i]) for i, (a, b) in enumerate(copies)]
    for c in running:
        c.start()
    for c in running:
        c.wait()


def laid_out(where_ref, mine_ref, came_ref, own_ref, send_ref, staged, sems):
    side, core = where_ref[0], where_ref[1]
    half, rows = came_ref.shape[1], came_ref.shape[2]
    mine = pl.multiple_of(core * rows, rows)
    other = pl.multiple_of((1 - core) * rows, rows)
    finish(
        [(mine_ref, staged.at[:, :, pl.ds(mine, rows)]), (came_ref, staged.at[:, :, pl.ds(other, rows)])], sems
    )
    quarter = half // 2
    heads = [pl.ds(who * quarter, quarter) for who in (side, 1 - side)]
    finish([(staged.at[:, at], to) for at, to in zip(heads, (own_ref, send_ref))], sems)


def lay_out(here, mine, came):
    _, half, rows, dim = came.shape
    return pl.pallas_call(
        laid_out,
        in_specs=[pl.BlockSpec(memory_space=pltpu.SMEM)] + [pl.BlockSpec(memory_space=pl.ANY)] * 2,
        out_specs=[pl.BlockSpec(memory_space=pl.ANY)] * 2,
        out_shape=[jax.ShapeDtypeStruct((2, half // 2, 2 * rows, dim), came.dtype)] * 2,
        scratch_shapes=[pltpu.VMEM((2, half, 2 * rows, dim), came.dtype), pltpu.SemaphoreType.DMA((2,))],
        compiler_params=pltpu.CompilerParams(vmem_limit_bytes=SMALL),
        cost_estimate=pl.CostEstimate(flops=0, bytes_accessed=8 * half * rows * dim * 2, transcendentals=0),
    )(here, mine, came)


def gathered(where_ref, *refs, sizes):
    n = len(sizes)
    runs = [refs[4 * j : 4 * j + 4] for j in range(n)]
    results, sems = refs[4 * n : 4 * n + 2], refs[-1]
    side, core = where_ref[0], where_ref[1]
    quarter = sum(sizes)
    rows = results[0].shape[1]
    mine = pl.ds(pl.multiple_of(core * rows, rows), rows)
    copies = []
    for (begin, size), run in zip(zip(starts(sizes), sizes), runs):
        for k, ref in enumerate(run):
            which_core, which_side = (core, 1 - core)[k % 2], (side, 1 - side)[k // 2]
            at = pl.ds(which_core * 2 * quarter + which_side * quarter + begin, size)
            for i, to in enumerate(results):
                copies.append((ref.at[i, :, mine] if k >= 2 else ref.at[i], to.at[at]))
    finish(copies, sems)


def gather(here, runs):
    sizes = tuple(run[0].shape[1] for run in runs)
    _, _, rows, dim = runs[0][0].shape
    shape = (4 * sum(sizes), rows, dim)
    return pl.pallas_call(
        functools.partial(gathered, sizes=sizes),
        grid=(1,),
        in_specs=[pl.BlockSpec(memory_space=pltpu.SMEM)] + [whole(x.shape) for run in runs for x in run],
        out_specs=[pl.BlockSpec(memory_space=pl.ANY)] * 2,
        out_shape=[jax.ShapeDtypeStruct(shape, runs[0][0].dtype)] * 2,
        scratch_shapes=[pltpu.SemaphoreType.DMA((8 * len(sizes),))],
        compiler_params=pltpu.CompilerParams(vmem_limit_bytes=SMALL),
        cost_estimate=pl.CostEstimate(flops=0, bytes_accessed=16 * sum(sizes) * rows * dim * 2, transcendentals=0),
    )(here, *[x for run in runs for x in run])


def tied(x, *after):
    return lax.optimization_barrier((x,) + after)[0] if after else x


def local(query_in, key_in, value_in, grad_out, doc_ids, frame_kind):
    rows_own, heads, dim = query_in.shape
    half = heads // 2
    span = 2 * rows_own
    count = lax.axis_size("ctx") * lax.axis_size("head")
    at = lax.axis_index("ctx") * lax.axis_size("head") + lax.axis_index("head")
    core = at % 2
    side = (at // 2) % 2
    base = (at - at % GROUP) * rows_own
    scale = dim**-0.5
    here = jnp.stack([side, core]).astype(jnp.int32)

    def sent(x, pairs, name):
        with jax.named_scope(name):
            return lax.ppermute(x, AXES, [(i, j) for i, j in pairs if 0 <= j < count])

    ahead = [(i, i + GROUP) for i in range(count)]
    behind = [(i, i - GROUP) for i in range(count)]
    across = [(i, i ^ 1) for i in range(count)]
    beside = [(i, i ^ 2) for i in range(count)]

    by_head = [x.transpose(1, 0, 2) for x in (key_in, value_in, query_in, grad_out)]

    def halves(x, y, which):
        return jnp.stack([lax.dynamic_slice_in_dim(a, which * half, half, 0) for a in (x, y)])

    quarter = half // 2
    cuts = tuple(zip(starts(CHUNKS), CHUNKS))
    came_kv = sent(halves(*by_head[:2], 1 - core), across, "pair_kv")
    kv_own, kv_send = lay_out(here, halves(*by_head[:2], core), came_kv)
    past_own = sent(kv_own, ahead, "far_kv_own")
    kv_beside = sent(kv_send, beside, "side_kv")
    came_q = sent(tied(halves(*by_head[2:], 1 - core), came_kv), across, "pair_q")
    q_own, q_send = lay_out(here, halves(*by_head[2:], core), came_q)
    past_beside = sent(tied(kv_beside, q_own, past_own), ahead, "far_kv_beside")
    q_beside = sent(tied(q_send, kv_beside), beside, "side_q")

    doc_ids, frame_kind = tied((doc_ids, frame_kind), came_q)
    reach = GROUP * rows_own
    docs = jnp.concatenate(
        [jnp.full((reach,), -1, jnp.int32), doc_ids, jnp.full((reach,), -2, jnp.int32)]
    )
    docs = lax.dynamic_slice_in_dim(docs, base, 3 * reach)
    kinds = lax.dynamic_slice_in_dim(frame_kind, base // FRAME, reach // FRAME)
    place = jnp.arange(reach, dtype=jnp.int32)
    limit = jnp.where(jnp.repeat(kinds, FRAME) == 1, (place // FRAME) * FRAME + FRAME - 1, place)
    rows = jnp.stack([docs[reach:], jnp.concatenate([limit, limit])])
    cols = rows[:, :reach].T
    key_docs = docs[None, : 2 * reach]

    pieces, coming = [], []
    for start, size in cuts:
        pick = slice(start, start + size)
        both = jnp.concatenate([q_own[:, pick], q_beside[:, pick]], axis=1)
        pieces.append(both)

    def returned(keep, theirs, came, name, *after):
        return keep, sent(tied(theirs, *after), across, "pair_" + name), came, sent(tied(came, *after), across, "pair_of_" + name)

    arrays = [(x, 0) for x in (q_own, q_beside, kv_own, kv_beside, past_own, past_beside)]
    *found, stats = attend(forward_kernel, quarter, here, arrays, [], [cols, key_docs], scale, True)
    out_came = sent(found[2], beside, "side_out")
    runs = []
    next_stats = None
    for j, (start, size) in enumerate(cuts):
        after = [next_stats] if j else [past_beside]
        if j >= 2:
            after.append(runs[0][0])
        coming.append(sent(tied(pieces[j], *after), behind, f"far_q_{start}"))
        if j == 0:
            next_stats = sent(tied(stats, coming[0]), behind, "far_stats")
        x = coming[j]
        arrays = [(a, start) for a in (kv_own, kv_beside, q_own, q_beside)] + [(x, 0), (x, size)]
        at = tied(here, results[0]) if j == GATHER_BEFORE else here
        grads = attend(
            backward_kernel, size, at, arrays, [(stats, start), (next_stats, start)], [cols, rows], scale, False
        )
        if j == 0:
            results = list(gather(tied(here, grads[0]), [returned(*found[:2], out_came, "out", grads[0])]))
        came = sent(grads[2], beside, f"side_grads_{start}")
        runs.append(returned(*grads[:2], came, f"grads_{start}"))
    results += list(gather(here, runs))
    return tuple(x.transpose(1, 0, 2) for x in results)


def solution(mesh):
    placed = P(AXES, None, None)
    return jax.shard_map(
        local,
        mesh=mesh,
        in_specs=(placed,) * 4 + (P(), P()),
        out_specs=(placed,) * 4,
        check_vma=False,
    )
```

```python
import functools
import math

import jax
import jax.numpy as jnp
from jax import lax
from jax.experimental import pallas as pl
from jax.experimental.pallas import tpu as pltpu
from jax.sharding import PartitionSpec as P

FRAME = 64
AXES = ("ctx", "head")
GROUP = 4
MASKED = -1e30
CHUNKS = (2, 2, 1)
COST = 0.1
GATHER_BEFORE = 2
VMEM = 16 * 2**20
SMALL = 8 * 2**20
NT = ((1,), (1,))
NN = ((1,), (0,))


def dot(a, b, dims):
    return lax.dot_general(a, b, (dims, ((), ())), preferred_element_type=jnp.float32)


def starts(sizes):
    return [sum(sizes[:i]) for i in range(len(sizes))]


def placed(done, side, core, keep_ref, theirs_ref, send_ref):
    rows = keep_ref.shape[2]
    mine = pl.multiple_of(core * rows, rows)
    other = pl.multiple_of((1 - core) * rows, rows)
    keep_ref[:, 0] = done[side, :, pl.ds(mine, rows), :]
    theirs_ref[:, 0] = done[side, :, pl.ds(other, rows), :]
    send_ref[:, 0] = done[1 - side]


def ordered(side, own_ref, beside_ref):
    first, second = [], []
    for i in range(2):
        own, beside = own_ref[i, 0], beside_ref[i, 0]
        first.append(jnp.where(side == 0, own, beside))
        second.append(jnp.where(side == 0, beside, own))
    return [tuple(first), tuple(second)]


def forward_kernel(
    where_ref, q_own, q_beside, kv_own, kv_beside, past_own, past_beside, cols_ref, docs_ref,
    keep_ref, theirs_ref, send_ref, stat_ref, done, *, scale
):
    span = q_own.shape[2]
    factor = scale * math.log2(math.e)
    side, core = where_ref[0], where_ref[1]
    queries = ordered(side, q_own, q_beside)
    blocks = ordered(side, past_own, past_beside) + ordered(side, kv_own, kv_beside)
    for part in range(2):
        query, grad = queries[part]
        at = part * span
        doc_col, limit_col = cols_ref[at : at + span, 0:1], cols_ref[at : at + span, 1:2]
        segments = blocks[part : part + 3]
        scores = []
        for i, (key, _) in enumerate(segments):
            raw = dot(query, key, NT) * factor
            allowed = docs_ref[:, at + i * span : at + (i + 1) * span] == doc_col
            if i == 2:
                place = at + lax.broadcasted_iota(jnp.int32, raw.shape, 1)
                allowed = allowed & (place <= limit_col)
            scores.append(jnp.where(allowed, raw, MASKED))
        top = functools.reduce(jnp.maximum, [jnp.max(s, axis=1, keepdims=True) for s in scores])
        raised = [jnp.exp2(s - top) for s in scores]
        total = functools.reduce(jnp.add, [jnp.sum(r, axis=1, keepdims=True) for r in raised])
        inverse = 1.0 / total
        probs = [r * inverse for r in raised]
        mixed = functools.reduce(
            jnp.add, [dot(p.astype(jnp.bfloat16), value, NN) for (_, value), p in zip(segments, probs)]
        )
        output = mixed.astype(jnp.bfloat16)
        delta = jnp.sum(grad.astype(jnp.float32) * output.astype(jnp.float32), axis=1, keepdims=True)
        grad_query = jnp.zeros_like(mixed)
        for (key, value), p in zip(segments, probs):
            grad_score = (p * (dot(grad, value, NT) - delta)).astype(jnp.bfloat16)
            grad_query += dot(grad_score, key, NN)
        done[part, 0] = output
        done[part, 1] = (grad_query * scale).astype(jnp.bfloat16)
        for i, column in enumerate((top + jnp.log2(total), delta)):
            stat_ref[0, i : i + 1, at : at + span] = jnp.broadcast_to(column, (span, 128)).T[0:1]
    placed(done, side, core, keep_ref, theirs_ref, send_ref)


def backward_kernel(
    where_ref, kv_own, kv_beside, q_own, q_beside, next_own, next_beside, stat_ref, next_stat_ref, cols_ref, rows_ref,
    keep_ref, theirs_ref, send_ref, done, *, scale
):
    span = kv_own.shape[2]
    factor = scale * math.log2(math.e)
    side, core = where_ref[0], where_ref[1]
    keys = ordered(side, kv_own, kv_beside)
    blocks = ordered(side, q_own, q_beside) + ordered(side, next_own, next_beside)
    for part in range(2):
        key, value = keys[part]
        at = part * span
        key_doc = cols_ref[at : at + span, 0:1]
        grad_key = jnp.zeros(key.shape, jnp.float32)
        grad_value = jnp.zeros(key.shape, jnp.float32)
        for i in range(3):
            query, grad = blocks[part + i]
            block = part + i
            lo = block * span
            stats = stat_ref if block < 2 else next_stat_ref
            here = (block % 2) * span
            raw = dot(key, query, NT) * factor
            allowed = key_doc == rows_ref[0:1, lo : lo + span]
            if i == 0:
                place = at + lax.broadcasted_iota(jnp.int32, raw.shape, 0)
                allowed = allowed & (place <= rows_ref[1:2, lo : lo + span])
            probs = jnp.exp2(jnp.where(allowed, raw - stats[0, 0:1, here : here + span], MASKED))
            grad_value += dot(probs.astype(jnp.bfloat16), grad, NN)
            grad_prob = dot(value, grad, NT)
            grad_score = (probs * (grad_prob - stats[0, 1:2, here : here + span])).astype(jnp.bfloat16)
            grad_key += dot(grad_score, query, NN)
        done[part, 0] = (grad_key * scale).astype(jnp.bfloat16)
        done[part, 1] = grad_value.astype(jnp.bfloat16)
    placed(done, side, core, keep_ref, theirs_ref, send_ref)


def per_head(shape, start=0):
    return pl.BlockSpec((shape[0], 1) + shape[2:], lambda h: (0, h + start, 0, 0))


def per_head_stats(shape, start=0):
    return pl.BlockSpec((1,) + shape[1:], lambda h: (h + start, 0, 0))


def whole(shape):
    return pl.BlockSpec(shape, lambda h: (0,) * len(shape))


def cost(heads, span, dim):
    pairs = heads * span * span * 3
    return pl.CostEstimate(
        flops=int(COST * 2 * pairs * dim * 4), bytes_accessed=int(COST * heads * span * dim * 2 * 10), transcendentals=int(COST * pairs)
    )


def attend(kernel, heads, here, arrays, stats, tables, scale, gives_stats):
    _, _, span, dim = arrays[0][0].shape
    rows = span // 2
    shapes = [(2, heads, rows, dim), (2, heads, rows, dim), (2, heads, span, dim)]
    out_specs = [per_head(shape) for shape in shapes]
    out_shape = [jax.ShapeDtypeStruct(shape, jnp.bfloat16) for shape in shapes]
    if gives_stats:
        out_specs.append(per_head_stats((heads, 2, 2 * span)))
        out_shape.append(jax.ShapeDtypeStruct((heads, 2, 2 * span), jnp.float32))
    return pl.pallas_call(
        functools.partial(kernel, scale=scale),
        grid=(heads,),
        in_specs=[pl.BlockSpec(memory_space=pltpu.SMEM)]
        + [per_head(x.shape, first) for x, first in arrays]
        + [per_head_stats(x.shape, first) for x, first in stats]
        + [whole(x.shape) for x in tables],
        out_specs=out_specs,
        out_shape=out_shape,
        scratch_shapes=[pltpu.VMEM((2, 2, span, dim), jnp.bfloat16)],
        compiler_params=pltpu.CompilerParams(vmem_limit_bytes=VMEM),
        cost_estimate=cost(2 * heads, span, dim),
    )(here, *[x for x, _ in arrays], *[x for x, _ in stats], *tables)


def finish(copies, sems):
    running = [pltpu.make_async_copy(a, b, sems.at[i]) for i, (a, b) in enumerate(copies)]
    for c in running:
        c.start()
    for c in running:
        c.wait()


def laid_out(where_ref, mine_ref, came_ref, own_ref, send_ref, staged, sems):
    side, core = where_ref[0], where_ref[1]
    half, rows = came_ref.shape[1], came_ref.shape[2]
    mine = pl.multiple_of(core * rows, rows)
    other = pl.multiple_of((1 - core) * rows, rows)
    finish(
        [(mine_ref, staged.at[:, :, pl.ds(mine, rows)]), (came_ref, staged.at[:, :, pl.ds(other, rows)])], sems
    )
    quarter = half // 2
    heads = [pl.ds(who * quarter, quarter) for who in (side, 1 - side)]
    finish([(staged.at[:, at], to) for at, to in zip(heads, (own_ref, send_ref))], sems)


def lay_out(here, mine, came):
    _, half, rows, dim = came.shape
    return pl.pallas_call(
        laid_out,
        in_specs=[pl.BlockSpec(memory_space=pltpu.SMEM)] + [pl.BlockSpec(memory_space=pl.ANY)] * 2,
        out_specs=[pl.BlockSpec(memory_space=pl.ANY)] * 2,
        out_shape=[jax.ShapeDtypeStruct((2, half // 2, 2 * rows, dim), came.dtype)] * 2,
        scratch_shapes=[pltpu.VMEM((2, half, 2 * rows, dim), came.dtype), pltpu.SemaphoreType.DMA((2,))],
        compiler_params=pltpu.CompilerParams(vmem_limit_bytes=SMALL),
        cost_estimate=pl.CostEstimate(flops=0, bytes_accessed=8 * half * rows * dim * 2, transcendentals=0),
    )(here, mine, came)


def gathered(where_ref, *refs, sizes):
    n = len(sizes)
    runs = [refs[4 * j : 4 * j + 4] for j in range(n)]
    results, sems = refs[4 * n : 4 * n + 2], refs[-1]
    side, core = where_ref[0], where_ref[1]
    quarter = sum(sizes)
    rows = results[0].shape[1]
    mine = pl.ds(pl.multiple_of(core * rows, rows), rows)
    copies = []
    for (begin, size), run in zip(zip(starts(sizes), sizes), runs):
        for k, ref in enumerate(run):
            which_core, which_side = (core, 1 - core)[k % 2], (side, 1 - side)[k // 2]
            at = pl.ds(which_core * 2 * quarter + which_side * quarter + begin, size)
            for i, to in enumerate(results):
                copies.append((ref.at[i, :, mine] if k >= 2 else ref.at[i], to.at[at]))
    finish(copies, sems)


def gather(here, runs):
    sizes = tuple(run[0].shape[1] for run in runs)
    _, _, rows, dim = runs[0][0].shape
    shape = (4 * sum(sizes), rows, dim)
    return pl.pallas_call(
        functools.partial(gathered, sizes=sizes),
        grid=(1,),
        in_specs=[pl.BlockSpec(memory_space=pltpu.SMEM)] + [whole(x.shape) for run in runs for x in run],
        out_specs=[pl.BlockSpec(memory_space=pl.ANY)] * 2,
        out_shape=[jax.ShapeDtypeStruct(shape, runs[0][0].dtype)] * 2,
        scratch_shapes=[pltpu.SemaphoreType.DMA((8 * len(sizes),))],
        compiler_params=pltpu.CompilerParams(vmem_limit_bytes=SMALL),
        cost_estimate=pl.CostEstimate(flops=0, bytes_accessed=16 * sum(sizes) * rows * dim * 2, transcendentals=0),
    )(here, *[x for run in runs for x in run])


def tied(x, *after):
    return lax.optimization_barrier((x,) + after)[0] if after else x


def local(query_in, key_in, value_in, grad_out, doc_ids, frame_kind):
    rows_own, heads, dim = query_in.shape
    half = heads // 2
    span = 2 * rows_own
    count = lax.axis_size("ctx") * lax.axis_size("head")
    at = lax.axis_index("ctx") * lax.axis_size("head") + lax.axis_index("head")
    core = at % 2
    side = (at // 2) % 2
    base = (at - at % GROUP) * rows_own
    scale = dim**-0.5
    here = jnp.stack([side, core]).astype(jnp.int32)

    def sent(x, pairs, name):
        with jax.named_scope(name):
            return lax.ppermute(x, AXES, [(i, j) for i, j in pairs if 0 <= j < count])

    ahead = [(i, i + GROUP) for i in range(count)]
    behind = [(i, i - GROUP) for i in range(count)]
    across = [(i, i ^ 1) for i in range(count)]
    beside = [(i, i ^ 2) for i in range(count)]

    by_head = [x.transpose(1, 0, 2) for x in (key_in, value_in, query_in, grad_out)]

    def halves(x, y, which):
        return jnp.stack([lax.dynamic_slice_in_dim(a, which * half, half, 0) for a in (x, y)])

    quarter = half // 2
    cuts = tuple(zip(starts(CHUNKS), CHUNKS))
    came_kv = sent(halves(*by_head[:2], 1 - core), across, "pair_kv")
    kv_own, kv_send = lay_out(here, halves(*by_head[:2], core), came_kv)
    past_own = sent(kv_own, ahead, "far_kv_own")
    kv_beside = sent(kv_send, beside, "side_kv")
    q_in, g_in = tied(tuple(by_head[2:]), kv_own)
    came_q = sent(halves(q_in, g_in, 1 - core), across, "pair_q")
    q_own, q_send = lay_out(here, halves(q_in, g_in, core), came_q)
    past_beside = sent(tied(kv_beside, past_own), ahead, "far_kv_beside")
    q_beside = sent(tied(q_send, kv_beside), beside, "side_q")

    doc_ids, frame_kind = tied((doc_ids, frame_kind), came_q)
    reach = GROUP * rows_own
    docs = jnp.concatenate(
        [jnp.full((reach,), -1, jnp.int32), doc_ids, jnp.full((reach,), -2, jnp.int32)]
    )
    docs = lax.dynamic_slice_in_dim(docs, base, 3 * reach)
    kinds = lax.dynamic_slice_in_dim(frame_kind, base // FRAME, reach // FRAME)
    place = jnp.arange(reach, dtype=jnp.int32)
    limit = jnp.where(jnp.repeat(kinds, FRAME) == 1, (place // FRAME) * FRAME + FRAME - 1, place)
    rows = jnp.stack([docs[reach:], jnp.concatenate([limit, limit])])
    cols = rows[:, :reach].T
    key_docs = docs[None, : 2 * reach]

    pieces, coming = [], []
    for start, size in cuts:
        pick = slice(start, start + size)
        both = jnp.concatenate([q_own[:, pick], q_beside[:, pick]], axis=1)
        pieces.append(both)

    def returned(keep, theirs, came, name, *after):
        return keep, sent(tied(theirs, *after), across, "pair_" + name), came, sent(tied(came, *after), across, "pair_of_" + name)

    arrays = [(x, 0) for x in (q_own, q_beside, kv_own, kv_beside, past_own, past_beside)]
    *found, stats = attend(forward_kernel, quarter, here, arrays, [], [cols, key_docs], scale, True)
    out_came = sent(found[2], beside, "side_out")
    runs = []
    next_stats = None
    for j, (start, size) in enumerate(cuts):
        after = [next_stats] if j else [past_beside]
        if j >= 2:
            after.append(runs[0][0])
        coming.append(sent(tied(pieces[j], *after), behind, f"far_q_{start}"))
        if j == 0:
            next_stats = sent(tied(stats, coming[0]), behind, "far_stats")
        x = coming[j]
        arrays = [(a, start) for a in (kv_own, kv_beside, q_own, q_beside)] + [(x, 0), (x, size)]
        at = tied(here, results[0]) if j == GATHER_BEFORE else here
        grads = attend(
            backward_kernel, size, at, arrays, [(stats, start), (next_stats, start)], [cols, rows], scale, False
        )
        if j == 0:
            results = list(gather(tied(here, grads[0]), [returned(*found[:2], out_came, "out", grads[0])]))
        came = sent(grads[2], beside, f"side_grads_{start}")
        runs.append(returned(*grads[:2], came, f"grads_{start}"))
    results += list(gather(here, runs))
    return tuple(x.transpose(1, 0, 2) for x in results)


def solution(mesh):
    placed = P(AXES, None, None)
    return jax.shard_map(
        local,
        mesh=mesh,
        in_specs=(placed,) * 4 + (P(), P()),
        out_specs=(placed,) * 4,
        check_vma=False,
    )
```
